128 devices in a mesh: layer: 4 (over y_hi, core), tok: 32 (over y_lo, z, x).
Axes of the slice: x: 4, y: 4 (y_hi: 2, y_lo: 2; y = y_hi * 2 + y_lo), z: 4, core: 2. Of those that a mesh axis runs over, the one named last changes fastest.
Arguments:
- inputs: bfloat16 [8, 20480, 4096], P('layer', 'tok'), may hold values from -6 to 6
- out_grads: bfloat16 [8, 20480, 4096], P('layer', 'tok'), may hold values from -6 to 6
- a_inverse: bfloat16 [8, 4096, 4096], P('layer', None, 'tok'), as said below
- g_inverse: bfloat16 [8, 4096, 4096], P('layer', None, 'tok'), as said below
- query_in: bfloat16 [8, 32, 8, 4096], P('layer', None, None, 'tok'), may hold values from -0.03125 to 0.03125
- query_out: bfloat16 [8, 32, 8, 4096], P('layer', None, None, 'tok'), may hold values from -0.03125 to 0.03125
Outputs:
- scores: float32 [20480, 32], P('tok', 'layer')
The draws below stay inside these ranges and needn't reach their ends.
Inputs may be any that keep to these rules, and one draw needn't show every extreme that they name: `a_inverse`: each layer's factor is the identity plus independent entries of deviation D ** -0.5. `g_inverse`: each layer's factor is the identity plus independent entries of deviation D ** -0.5.
All inputs are finite; a program needn't handle non-finite values.
Results may differ from the reference program's by a relative error of at most 0.0041.
Values may be sent and summed in bfloat16 or wider, within the bound.
A program may use at most 128 MiB of HBM per device.

```python
import jax
import jax.numpy as jnp

D = 4096
RANK = 8
LAYERS = 8
TOKENS = 20480
QUERIES = 32


def factor_draw(key, salt):
    noise = jax.random.normal(jax.random.fold_in(key, salt), (LAYERS, D, D), jnp.float32) * D ** (-0.5)
    return (noise + jnp.eye(D, dtype=jnp.float32)[None]).astype(jnp.bfloat16)


def draw_a_inverse(key, part):
    return factor_draw(key, 11)


def draw_g_inverse(key, part):
    return factor_draw(key, 23)


def steps_of(stream_key, extent, shards, smallest, largest):
    factor_of, own = 1.0, jax.random.fold_in(stream_key, 6)
    for position, shards_of in shards:
        heights = jnp.exp(jax.random.uniform(jax.random.fold_in(own, position), (shards_of,), jnp.float32, smallest / len(shards), largest / len(shards)))
        factor_of = factor_of * jnp.repeat(heights, extent[position] // shards_of).reshape([-1 if axis == position else 1 for axis in range(len(extent))])
    return factor_of


def scatter_about(rng, shape, deviation, bound, shards=(), kind=jnp.bfloat16):
    loudness = steps_of(rng, shape, shards, -0.22, 0.18) if shards else 1.0
    drawn = jax.random.normal(rng, shape, jnp.float32) * deviation * loudness
    return jnp.minimum(jnp.maximum(drawn, -bound), bound).astype(kind)


def setup_inputs(seed: int = 0) -> dict:
    seeds = jax.random.split(jax.random.key(seed), 7)
    inputs = scatter_about(seeds[0], (LAYERS, TOKENS, D), 1.0, 6.0, ((0, 4), (1, 32)))
    out_grads = scatter_about(seeds[1], (LAYERS, TOKENS, D), 1.0, 6.0, ((0, 4), (1, 32)))
    a_inverse = draw_a_inverse(jax.random.fold_in(seeds[6], 71), 0)
    g_inverse = draw_g_inverse(jax.random.fold_in(seeds[6], 71), 0)
    query_in = scatter_about(seeds[4], (LAYERS, QUERIES, RANK, D), (8 * D) ** -0.5, 0.03125, ((0, 4), (3, 32)))
    query_out = scatter_about(seeds[5], (LAYERS, QUERIES, RANK, D), (8 * D) ** -0.5, 0.03125, ((0, 4), (3, 32)))
    return {"inputs": inputs, "out_grads": out_grads, "a_inverse": a_inverse, "g_inverse": g_inverse, "query_in": query_in, "query_out": query_out}


def reference(inputs, out_grads, a_inverse, g_inverse, query_in, query_out):
    scores = jnp.zeros((inputs.shape[1], query_in.shape[1]), jnp.float32)
    for layer_no in range(inputs.shape[0]):
        pre_in = jnp.einsum("qrj,ij->qri", query_in[layer_no], a_inverse[layer_no], preferred_element_type=jnp.float32).astype(jnp.bfloat16)
        pre_out = jnp.einsum("qrj,ij->qri", query_out[layer_no], g_inverse[layer_no], preferred_element_type=jnp.float32).astype(jnp.bfloat16)
        side_in = jnp.einsum("td,qrd->tqr", inputs[layer_no], pre_in, preferred_element_type=jnp.float32)
        side_out = jnp.einsum("td,qrd->tqr", out_grads[layer_no], pre_out, preferred_element_type=jnp.float32)
        scores = scores + jnp.sum(side_in * side_out, axis=2)
    return scores
```

```python
import functools

import jax
import jax.numpy as jnp
from jax import lax
from jax.experimental import pallas as pl
from jax.experimental.pallas import tpu as pltpu
from jax.sharding import PartitionSpec as P

MESH = pl.DeviceIdType.MESH
BF16, F32 = jnp.bfloat16, jnp.float32
SCALE = 2.0**29
NT = (((1,), (1,)), ((), ()))
SLABS = 4


def encode(v):
    a = v * jnp.abs(v)
    return (a * jnp.abs(a)).astype(BF16)


def decode(code):
    w = code.astype(F32)
    r = lax.rsqrt(jnp.maximum(jnp.abs(w), 1e-37))
    return w * (r * r * lax.rsqrt(r))


def order():
    todo = []
    for s in range(SLABS):
        for k in range(11):
            for b in range(2):
                todo.append((START[s] + GAP[k], s, b, k))
    return [(s, b, k) for _, s, b, k in sorted(todo)]


START = (0, 8, 16, 24)
GAP = (0, 4, 6, 8, 9.5, 11, 12.5, 14, 15.5, 20, 23)


def kernel(
    q_ref, a_hbm, g_hbm, x_hbm, o_hbm, out_ref,
    qs, fac, inp, part_a, part_b, pre_a, pre_b,
    rp_a, rs_a, ry_a, ry_b, rs_b, rp_b,
    sp_a, ss_a, sy_a, sy_b, ss_b, sp_b,
    side, fin, rfin,
    fac_sem, inp_sem, send_sem, recv_sem, fin_send, fin_recv,
):
    lay, tok = lax.axis_index("layer"), lax.axis_index("tok")
    core = lay % 2
    y = tok // 16
    step_p, step_s = 1 + 3 * core, 4 - 3 * core
    p, s = (tok // step_p) % 4, (tok // step_s) % 4
    ha, qb = part_a.shape[-1], part_b.shape[-1]
    wa = 2 * ha

    def at(p_, s_, y_):
        return (lay, y_ * 16 + p_ * step_p + s_ * step_s)

    right_p, left_p = at((p + 1) % 4, s, y), at((p + 3) % 4, s, y)
    right_s, left_s = at(p, (s + 1) % 4, y), at(p, (s + 3) % 4, y)
    across = at(p, s, 1 - y)
    peers = [((lay + d) % 4, tok) for d in (1, 2, 3)]

    def fac_copy(k):
        src = (a_hbm, g_hbm)[k % 2]
        return pltpu.make_async_copy(src.at[k // 2], fac.at[k], fac_sem.at[k])

    def inp_copy(k):
        src = (x_hbm, o_hbm)[k % 2]
        return pltpu.make_async_copy(src.at[k // 2], inp.at[k % 2], inp_sem.at[k])

    for k in range(SLABS):
        fac_copy(k).start()
    for k in range(2):
        inp_copy(k).start()

    barrier = pltpu.get_barrier_semaphore()
    everyone = [right_p, left_p, right_s, left_s, across, *peers]
    for who in everyone:
        pl.semaphore_signal(barrier, inc=1, device_id=who, device_id_type=MESH)

    qs[...] = q_ref[...] * jnp.asarray(SCALE, BF16)

    def partial_products(k):
        def tile(dst, row, width):
            dst[...] = lax.dot_general(
                qs[k], fac[k, pl.ds(row, width), :], NT, preferred_element_type=F32
            )

        for h in range(2):
            for c in range(0, ha, 512):
                tile(part_a.at[k, h, :, pl.ds(c, 512)], h * ha + c, 512)
        for h in range(4):
            tile(part_b.at[k, h // 2, h % 2], wa + h * qb, qb)

    def remote(k, b, n, src, dst, who):
        return pltpu.make_async_remote_copy(
            src_ref=src, dst_ref=dst, send_sem=send_sem.at[k, b, n], recv_sem=recv_sem.at[k, b, n],
            device_id=who, device_id_type=MESH,
        )

    def rows_loop(n, body):
        if n == 16:
            body(0)
        else:
            pl.loop(0, n // 16)(lambda i: body(pl.multiple_of(i * 16, 16)))

    def put(dst, src, row0, n, more=None):
        def body(r):
            v = src[pl.ds(pl.multiple_of(row0 + r, 16), 16), :]
            if more is not None:
                v = v + decode(more[pl.ds(r, 16), :])
            dst[pl.ds(r, 16), :] = encode(v)

        rows_loop(n, body)

    def add(src, row0, n, one, two=None):
        def body(r):
            rows = pl.ds(pl.multiple_of(row0 + r, 16), 16)
            v = src[rows, :] + decode(one[pl.ds(r, 16), :])
            if two is not None:
                v = v + decode(two[pl.ds(r, 16), :])
            src[rows, :] = v

        rows_loop(n, body)

    class Scatter:
        def __init__(self, k, b, base, halves, sent, got, row0, n, me, right, left):
            self.__dict__.update(locals())

        def copy(self, m):
            who = self.left if m % 2 else self.right
            return remote(self.k, self.b, self.base + m, self.sent.at[m], self.got.at[m], who)

        def row(self, d):
            return self.row0 + (self.me + d) % 4 * self.n

        def first(self):
            lo, hi = self.halves
            for m, (src, d) in enumerate(((hi, 2), (lo, 2), (lo, 1), (hi, 3))):
                put(self.sent.at[m], src, self.row(d), self.n)
                self.copy(m).start()

        def second(self):
            lo, hi = self.halves
            for m, (src, d) in enumerate(((hi, 1), (lo, 3))):
                self.copy(m).wait_recv()
                put(self.sent.at[4 + m], src, self.row(d), self.n, self.got.at[m])
                self.copy(4 + m).start()

        def last(self):
            lo, hi = self.halves
            for m in (2, 3, 4, 5):
                self.copy(m).wait_recv()
            add(lo, self.row(0), self.n, self.got.at[2], self.got.at[5])
            add(hi, self.row(0), self.n, self.got.at[3], self.got.at[4])

        def sends(self):
            return [self.copy(m) for m in range(6)]

    class Gather:
        def __init__(self, k, b, base, halves, row0, n, me, right, left):
            self.__dict__.update(locals())

        def copy(self, m):
            half = self.halves[(1, 0, 0, 1, 1, 0)[m]]
            d = (0, 0, 0, 0, 3, 1)[m]
            ref = half.at[pl.ds(pl.multiple_of(self.row0 + (self.me + d) % 4 * self.n, 16), self.n), :]
            return remote(self.k, self.b, self.base + m, ref, ref, self.left if m % 2 else self.right)

        def first(self):
            for m in range(4):
                self.copy(m).start()

        def second(self):
            for m in range(2):
                self.copy(m).wait_recv()
                self.copy(4 + m).start()

        def last(self):
            for m in (2, 3, 4, 5):
                self.copy(m).wait_recv()

        def sends(self):
            return [self.copy(m) for m in range(6)]

    def final_rows(dst, src, row0, n, got):
        rows = pl.ds(pl.multiple_of(row0, 16), n)
        dst[rows, :] = ((src[rows, :] + decode(got)) * (1.0 / SCALE)).astype(BF16)

    def ay_copy(k):
        return remote(k, 0, 12, sy_a.at[k], ry_a.at[k], across)

    def agy_copy(k):
        block = pre_a.at[k, y, pl.ds(pl.multiple_of(64 * p + 16 * s, 16), 16), :]
        return remote(k, 0, 13, block, block, across)

    def by_copy(k):
        return remote(k, 1, 12, sy_b.at[k], ry_b.at[k], across)

    def bgy_copy(k):
        block = pre_b.at[k, y]
        return remote(k, 1, 13, block, block, across)

    stage = {}
    for k in range(SLABS):
        ha_refs = [part_a.at[k, h] for h in range(2)]
        hb_refs = [part_b.at[k, y, h] for h in range(2)]
        ga_refs = [pre_a.at[k, h] for h in range(2)]
        gb_refs = [pre_b.at[k, y, h] for h in range(2)]
        stage[k] = dict(
            ap=Scatter(k, 0, 0, ha_refs, sp_a.at[k], rp_a.at[k], 0, 64, p, right_p, left_p),
            as_=Scatter(k, 0, 6, ha_refs, ss_a.at[k], rs_a.at[k], 64 * p, 16, s, right_s, left_s),
            ags=Gather(k, 0, 14, ga_refs, 64 * p, 16, s, right_s, left_s),
            agp=Gather(k, 0, 20, ga_refs, 0, 64, p, right_p, left_p),
            bs=Scatter(k, 1, 0, hb_refs, ss_b.at[k], rs_b.at[k], 0, 64, s, right_s, left_s),
            bp=Scatter(k, 1, 6, hb_refs, sp_b.at[k], rp_b.at[k], 64 * s, 16, p, right_p, left_p),
            bgp=Gather(k, 1, 14, gb_refs, 64 * s, 16, p, right_p, left_p),
            bgs=Gather(k, 1, 20, gb_refs, 0, 64, s, right_s, left_s),
        )

    def score(k, piece, first):
        acc = side.at[k % 2]
        data = inp.at[k % 2]

        def go(pre, col, width, init):
            v = lax.dot_general(data[:, pl.ds(col, width)], pre, NT, preferred_element_type=F32)
            acc[...] = v if init else acc[...] + v

        if piece == 0:
            for h in range(2):
                for c in range(0, ha, 512):
                    go(pre_a[k, h, :, pl.ds(c, 512)], h * ha + c, 512, first and h == 0 and c == 0)
        else:
            for h in range(4):
                go(pre_b[k, h // 2, h % 2], wa + h * qb, qb, first and h == 0)

    done = {}

    def finish(k, b):
        if k not in done:
            inp_copy(k).wait()
        score(k, b, k not in done)
        done[k] = done.get(k, 0) + 1
        if done[k] < 2:
            return
        if k + 2 < SLABS:
            inp_copy(k + 2).start()
        if k % 2:
            pick = jnp.where(
                lax.broadcasted_iota(jnp.int32, (32, 256), 1) // 8
                == lax.broadcasted_iota(jnp.int32, (32, 256), 0),
                1.0, 0.0,
            ).astype(BF16)
            for t in range(0, side.shape[1], 128):
                prod = side[0, pl.ds(t, 128), :] * side[1, pl.ds(t, 128), :]
                total = None
                for _ in range(3):
                    top = prod.astype(BF16)
                    prod = prod - top.astype(F32)
                    part = lax.dot_general(pick, top, NT, preferred_element_type=F32)
                    total = part if total is None else total + part
                fin[:, pl.ds(t, 128)] = total if k == 1 else fin[:, pl.ds(t, 128)] + total

    def a_step(k, n):
        g = stage[k]
        if n == 0:
            g["ap"].first()
        elif n == 1:
            g["ap"].second()
        elif n == 2:
            g["ap"].last()
            g["as_"].first()
        elif n == 3:
            g["as_"].second()
        elif n == 4:
            g["as_"].last()
            put(sy_a.at[k], part_a.at[k, 1 - y], 64 * p + 16 * s, 16)
            ay_copy(k).start()
        elif n == 5:
            ay_copy(k).wait_recv()
            final_rows(pre_a.at[k, y], part_a.at[k, y], 64 * p + 16 * s, 16, ry_a[k])
            agy_copy(k).start()
        elif n == 6:
            agy_copy(k).wait_recv()
            g["ags"].first()
        elif n == 7:
            g["ags"].second()
        elif n == 8:
            g["ags"].last()
            g["agp"].first()
        elif n == 9:
            g["agp"].second()
        else:
            g["agp"].last()
            finish(k, 0)

    def b_step(k, n):
        g = stage[k]
        if n == 0:
            for h in range(2):
                put(sy_b.at[k, h], part_b.at[k, 1 - y, h], 0, 256)
            by_copy(k).start()
        elif n == 1:
            by_copy(k).wait_recv()
            for h in range(2):
                add(part_b.at[k, y, h], 0, 256, ry_b.at[k, h])
            g["bs"].first()
        elif n == 2:
            g["bs"].second()
        elif n == 3:
            g["bs"].last()
            g["bp"].first()
        elif n == 4:
            g["bp"].second()
        elif n == 5:
            g["bp"].last()
            rows = pl.ds(pl.multiple_of(64 * s + 16 * p, 16), 16)
            for h in range(2):
                pre_b[k, y, h, rows, :] = (part_b[k, y, h, rows, :] * (1.0 / SCALE)).astype(BF16)
            g["bgp"].first()
        elif n == 6:
            g["bgp"].second()
        elif n == 7:
            g["bgp"].last()
            g["bgs"].first()
        elif n == 8:
            g["bgs"].second()
        elif n == 9:
            g["bgs"].last()
            bgy_copy(k).start()
        else:
            bgy_copy(k).wait_recv()
            finish(k, 1)

    met = False
    for k, b, n in order():
        if b == 0 and n == 0:
            fac_copy(k).wait()
            partial_products(k)
            if not met:
                pl.semaphore_wait(barrier, len(everyone))
                met = True
        (a_step, b_step)[b](k, n)

    def fin_copy(d):
        who = (lay + d) % 4
        return pltpu.make_async_remote_copy(
            src_ref=fin.at[pl.ds(pl.multiple_of(8 * who, 8), 8), :], dst_ref=rfin.at[d - 1],
            send_sem=fin_send.at[d - 1], recv_sem=fin_recv.at[d - 1],
            device_id=(who, tok), device_id_type=MESH,
        )

    for d in (2, 3, 1):
        fin_copy(d).start()
    for k in range(SLABS):
        g = stage[k]
        for ring in g.values():
            for c in ring.sends():
                c.wait_send()
        for c in (ay_copy(k), agy_copy(k), by_copy(k), bgy_copy(k)):
            c.wait_send()
    total = fin[pl.ds(pl.multiple_of(8 * lay, 8), 8), :]
    for d in (1, 2, 3):
        fin_copy(d).wait()
        total = total + rfin[d - 1]
    out_ref[...] = total


def local(inputs, out_grads, a_inverse, g_inverse, query_in, query_out):
    layers, tokens, width = inputs.shape
    depth = a_inverse.shape[2]
    rows = query_in.shape[1] * query_in.shape[2]
    wb = 1024
    ha, qb = (width - wb) // 2, wb // 4
    q = jnp.stack([query_in, query_out], axis=1).reshape(SLABS, rows, depth)
    vmem = pltpu.VMEM
    dma = pltpu.SemaphoreType.DMA
    coded = [
        vmem((SLABS, 6, 64, ha), BF16), vmem((SLABS, 6, 16, ha), BF16), vmem((SLABS, 16, ha), BF16),
        vmem((SLABS, 2, rows, qb), BF16), vmem((SLABS, 6, 64, qb), BF16), vmem((SLABS, 6, 16, qb), BF16),
    ]
    hbm = pl.BlockSpec(memory_space=pl.ANY)
    scores = pl.pallas_call(
        kernel,
        out_shape=jax.ShapeDtypeStruct((8, tokens), F32),
        in_specs=[pl.BlockSpec(memory_space=pltpu.VMEM), hbm, hbm, hbm, hbm],
        out_specs=pl.BlockSpec(memory_space=pltpu.VMEM),
        scratch_shapes=[
            vmem((SLABS, rows, depth), BF16),
            vmem((SLABS, width, depth), BF16),
            vmem((2, tokens, width), BF16),
            vmem((SLABS, 2, rows, ha), F32),
            vmem((SLABS, 2, 2, rows, qb), F32),
            vmem((SLABS, 2, rows, ha), BF16),
            vmem((SLABS, 2, 2, rows, qb), BF16),
            *coded, *coded,
            vmem((2, tokens, rows), F32),
            vmem((32, tokens), F32),
            vmem((3, 8, tokens), F32),
            dma((SLABS,)), dma((SLABS,)),
            dma((SLABS, 2, 26)), dma((SLABS, 2, 26)),
            dma((3,)), dma((3,)),
        ],
        compiler_params=pltpu.CompilerParams(
            collective_id=1, has_side_effects=True, vmem_limit_bytes=60 * 2**20
        ),
        cost_estimate=pl.CostEstimate(flops=6 * 10**9, bytes_accessed=26 * 10**6, transcendentals=0),
        name="influence",
    )(q, a_inverse, g_inverse, inputs, out_grads)
    return scores.T


def solution(mesh):
    in_specs = (
        P("layer", "tok", None),
        P("layer", "tok", None),
        P("layer", None, "tok"),
        P("layer", None, "tok"),
        P("layer", None, None, "tok"),
        P("layer", None, None, "tok"),
    )
    return jax.shard_map(
        local, mesh=mesh, in_specs=in_specs, out_specs=P("tok", "layer"), check_vma=False
    )
```

```python
import jax
import jax.numpy as jnp
from jax import lax
from jax.experimental import pallas as pl
from jax.experimental.pallas import tpu as pltpu
from jax.sharding import PartitionSpec as P

MESH = pl.DeviceIdType.MESH
BF16, F32 = jnp.bfloat16, jnp.float32
SCALE = 2.0**29
NT = (((1,), (1,)), ((), ()))
SLABS = 4
WEST, EAST = 3, 1

UNITS = (
    (0, 0, 0, 3072),
    (0, 1, 3072, 1024),
    (1, 0, 0, 2048),
    (1, 1, 2048, 1024),
    (1, 2, 3072, 1024),
    (2, 0, 0, 2048),
    (2, 1, 2048, 1024),
    (2, 2, 3072, 1024),
    (3, 0, 0, 2048),
    (3, 1, 2048, 1024),
    (3, 2, 3072, 1024),
)

ORDER = (
    0, 1, 2, 3, 4, 5, 6, 7, 8, 9, 10, 0, 1, 2, 1, 3, 5, 1, 4, 3, 8, 6, 3, 0, 2, 5, 6, 1, 4, 7,
    0, 2, 8, 9, 5, 3, 1, 4, 6, 7, 0, 2, 8, 10, 9, 3, 5, 1, 6, 7, 4, 8, 10, 0, 9, 3, 2, 1, 7, 4,
    5, 6, 10, 0, 8, 3, 9, 2, 7, 5, 6, 10, 0, 8, 2, 9, 5, 1, 4, 6, 10, 8, 9, 4, 0, 3, 7, 9, 4, 2,
    7, 5, 6, 10, 7, 8, 10, 9, 0, 4, 10, 2, 5, 7, 8, 4, 10, 7, 10,
)


def encode(v):
    a = v * jnp.abs(v)
    return (a * jnp.abs(a)).astype(BF16)


def decode(code):
    w = code.astype(F32)
    r = lax.rsqrt(jnp.maximum(jnp.abs(w), 1e-37))
    return w * (r * r * lax.rsqrt(r))


def aligned(row):
    return row if isinstance(row, int) else pl.multiple_of(row, 16)


class Remote:
    def __init__(self, log, sems, n, src, dst, who):
        self.log = log
        self.copy = pltpu.make_async_remote_copy(
            src_ref=src, dst_ref=dst, send_sem=sems[0].at[n], recv_sem=sems[1].at[n],
            device_id=who, device_id_type=MESH,
        )

    def start(self):
        self.copy.start()
        self.log.append(self.copy)

    def wait(self):
        self.copy.wait_recv()


def rows_loop(n, body):
    if n == 16:
        body(0)
    else:
        pl.loop(0, n // 16)(lambda i: body(pl.multiple_of(i * 16, 16)))


def put(dst, src, row0, n, more=None):
    def body(r):
        v = src[pl.ds(aligned(row0 + r), 16), :]
        if more is not None:
            v = v + decode(more[pl.ds(r, 16), :])
        dst[pl.ds(r, 16), :] = encode(v)

    rows_loop(n, body)


def add(src, row0, n, *coded):
    def body(r):
        rows = pl.ds(aligned(row0 + r), 16)
        v = src[rows, :]
        for c in coded:
            v = v + decode(c[pl.ds(r, 16), :])
        src[rows, :] = v

    rows_loop(n, body)


class Scatter:
    def __init__(self, remote, base, halves, sent, got, row0, n, me, ring):
        self.__dict__.update(locals())

    def copy(self, m):
        return self.remote(self.base + m, self.sent.at[m], self.got.at[m], self.ring[EAST if m % 2 == 0 else WEST])

    def row(self, d):
        return self.row0 + (self.me + d) % 4 * self.n

    def first(self):
        lo, hi = self.halves
        for m, (src, d) in enumerate(((hi, 2), (lo, 2), (lo, 1), (hi, 3))):
            put(self.sent.at[m], src, self.row(d), self.n)
            self.copy(m).start()

    def second(self):
        lo, hi = self.halves
        for m, (src, d) in enumerate(((hi, 1), (lo, 3))):
            self.copy(m).wait()
            put(self.sent.at[4 + m], src, self.row(d), self.n, self.got.at[m])
            self.copy(4 + m).start()

    def last(self):
        lo, hi = self.halves
        for m in (2, 3, 4, 5):
            self.copy(m).wait()
        add(lo, self.row(0), self.n, self.got.at[2], self.got.at[5])
        add(hi, self.row(0), self.n, self.got.at[3], self.got.at[4])


class Gather:
    def __init__(self, remote, base, halves, row0, n, me, ring):
        self.__dict__.update(locals())

    def copy(self, m):
        half = self.halves[(1, 0, 0, 1, 1, 0)[m]]
        d = (0, 0, 0, 0, 3, 1)[m]
        ref = half.at[pl.ds(aligned(self.row0 + (self.me + d) % 4 * self.n), self.n), :]
        return self.remote(self.base + m, ref, ref, self.ring[EAST if m % 2 == 0 else WEST])

    def first(self):
        for m in range(4):
            self.copy(m).start()

    def second(self):
        for m in range(2):
            self.copy(m).wait()
            self.copy(4 + m).start()

    def last(self):
        for m in (2, 3, 4, 5):
            self.copy(m).wait()


class Direct:
    def __init__(self, remote, base, halves, sent, got, row0, n, me, ring):
        self.__dict__.update(locals())

    def copy(self, m):
        return self.remote(self.base + m, self.sent.at[m], self.got.at[m], self.ring[(2, 1, 3)[m]])

    def first(self):
        for m, d in enumerate((2, 1, 3)):
            for h in range(2):
                put(self.sent.at[m, h], self.halves[h], self.row0 + (self.me + d) % 4 * self.n, self.n)
            self.copy(m).start()

    def last(self):
        for m in range(3):
            self.copy(m).wait()
        for h in range(2):
            add(self.halves[h], self.row0 + self.me * self.n, self.n, *[self.got.at[m, h] for m in range(3)])


class DirectGather:
    def __init__(self, remote, base, both, row0, n, me, ring):
        self.__dict__.update(locals())

    def copy(self, m):
        ref = self.both.at[:, pl.ds(aligned(self.row0 + self.me * self.n), self.n), :]
        return self.remote(self.base + m, ref, ref, self.ring[(2, 1, 3)[m]])

    def first(self):
        for m in range(3):
            self.copy(m).start()

    def last(self):
        for m in range(3):
            self.copy(m).wait()


def unit_scratch(kind, w):
    h, q = w // 2, w // 4
    if kind == 0:
        got = dict(first=(6, 64, h), second=(6, 16, h), y=(2, 16, h))
        own = dict(part=((2, 256, h), F32), pre=((2, 256, h), BF16))
    elif kind == 1:
        got = dict(first=(3, 2, 16, q), second=(6, 64, q))
        own = dict(part=((2, 256, q), F32), pre=((2, 2, 256, q), BF16), rows=((h, 128), BF16))
    else:
        got = dict(first=(6, 64, q), second=(6, 16, q))
        own = dict(part=((2, 256, q), F32), pre=((2, 256, h), BF16), rows=((h, 128), BF16))
    for name, shape in got.items():
        own["sent_" + name] = (shape, BF16)
        own["got_" + name] = (shape, BF16)
    own["send_sem"] = own["recv_sem"] = ((26,), None)
    return own


def kernel(qi_ref, qo_ref, a_hbm, g_hbm, x_hbm, o_hbm, out_ref, *scratch):
    (qs, qx, fac, inp, side, fin, rfin, fac_sem, inp_sem, q_send, q_recv, fin_send, fin_recv) = scratch[:13]
    rest = list(scratch[13:])
    bufs = [{name: rest.pop(0) for name in unit_scratch(kind, w)} for _, kind, _, w in UNITS]

    lay, tok = lax.axis_index("layer"), lax.axis_index("tok")
    core = lay % 2
    y = tok // 16
    step_p, step_s = 1 + 3 * core, 4 - 3 * core
    p, s = (tok // step_p) % 4, (tok // step_s) % 4

    def at(p_, s_, y_):
        return (lay, y_ * 16 + p_ * step_p + s_ * step_s)

    ring_p = [None] + [at((p + d) % 4, s, y) for d in (1, 2, 3)]
    ring_s = [None] + [at(p, (s + d) % 4, y) for d in (1, 2, 3)]
    across = at(p, s, 1 - y)
    peers = [((lay + d) % 4, tok) for d in (1, 2, 3)]

    def fac_copy(k):
        return pltpu.make_async_copy((a_hbm, g_hbm)[k % 2].at[k // 2], fac.at[k], fac_sem.at[k])

    def inp_copy(k):
        return pltpu.make_async_copy((x_hbm, o_hbm)[k % 2].at[k // 2], inp.at[k % 2], inp_sem.at[k])

    barrier = pltpu.get_barrier_semaphore()
    everyone = [*ring_p[1:], *ring_s[1:], across, *peers]
    for who in everyone:
        pl.semaphore_signal(barrier, inc=1, device_id=who, device_id_type=MESH)
    for k in range(SLABS):
        fac_copy(k).start()
    for k in range(2):
        inp_copy(k).start()
    for k in range(SLABS):
        qs[k] = (qi_ref, qo_ref)[k % 2][k // 2] * jnp.asarray(SCALE, BF16)

    log = []
    loaded, asked, arrived = set(), set(), set()

    def load(k):
        if k not in loaded:
            loaded.add(k)
            fac_copy(k).wait()

    def q_copy(k):
        return Remote(log, (q_send, q_recv), k, qs.at[k], qx.at[k], across)

    def dot(a, b):
        return lax.dot_general(a, b, NT, preferred_element_type=F32)

    waiting, scored = [], []

    def finish(u):
        waiting.append(u)
        for v in sorted(waiting):
            k = UNITS[v][0]
            if all(w in scored for w, unit in enumerate(UNITS) if unit[0] < k // 2 * 2):
                waiting.remove(v)
                take(v, k)

    def take(u, k):
        _, kind, col, w = UNITS[u]
        acc, data, pre = side.at[k % 2], inp.at[k % 2], bufs[u]["pre"]
        fresh = not any(UNITS[v][0] == k for v in scored)
        if fresh:
            inp_copy(k).wait()
        if kind == 1:
            pieces = [(pre[h // 2, h % 2], col + h * (w // 4), w // 4) for h in range(4)]
        else:
            pieces = [(pre[h], col + h * (w // 2), w // 2) for h in range(2)]
        for block, c, width in pieces:
            v = dot(data[:, pl.ds(c, width)], block)
            acc[...] = v if fresh else acc[...] + v
            fresh = False
        scored.append(u)
        if all(v in scored for v, unit in enumerate(UNITS) if unit[0] == k) and k + 2 < SLABS:
            inp_copy(k + 2).start()
        if all(v in scored for v, unit in enumerate(UNITS) if unit[0] // 2 == k // 2):
            layer_sum(k // 2)

    def layer_sum(layer):
        pick = jnp.where(
            lax.broadcasted_iota(jnp.int32, (32, 256), 1) // 8
            == lax.broadcasted_iota(jnp.int32, (32, 256), 0),
            1.0, 0.0,
        ).astype(BF16)
        for t in range(0, side.shape[1], 128):
            prod = side[0, pl.ds(t, 128), :] * side[1, pl.ds(t, 128), :]
            total = None
            for _ in range(3):
                top = prod.astype(BF16)
                prod = prod - top.astype(F32)
                part = dot(pick, top)
                total = part if total is None else total + part
            fin[:, pl.ds(t, 128)] = total if layer == 0 else fin[:, pl.ds(t, 128)] + total

    def exchange(u):
        k, _, col, w = UNITS[u]
        h = w // 2
        src = (a_hbm, g_hbm)[k % 2].at[k // 2, pl.ds(aligned(col + (1 - y) * h), h), :]
        return Remote(log, (bufs[u]["send_sem"], bufs[u]["recv_sem"]), 12, src, bufs[u]["rows"], across)

    def send_rows(u):
        k = UNITS[u][0]
        if k not in asked:
            asked.add(k)
            q_copy(k).start()
        exchange(u).start()

    def sum_rows(u):
        k, _, col, w = UNITS[u]
        load(k)
        if k not in arrived:
            arrived.add(k)
            q_copy(k).wait()
        exchange(u).wait()
        q, b = w // 4, bufs[u]
        for h in range(2):
            own = fac[k, pl.ds(aligned(col + y * (w // 2) + h * q), q), :]
            b["part"][h] = dot(qs[k], own) + dot(qx[k], b["rows"][pl.ds(h * q, q), :])

    def steps_of(u):
        k, kind, col, w = UNITS[u]
        b = bufs[u]
        part, pre, h, q = b["part"], b["pre"], w // 2, w // 4

        def remote(n, src, dst, who):
            return Remote(log, (b["send_sem"], b["recv_sem"]), n, src, dst, who)

        halves = [part.at[i] for i in range(2)]
        coded = lambda name: (b["sent_" + name], b["got_" + name])
        if kind == 0:
            one = Scatter(remote, 0, halves, *coded("first"), 0, 64, p, ring_p)
            two = Scatter(remote, 6, halves, *coded("second"), 64 * p, 16, s, ring_s)
            back_two = Gather(remote, 14, [pre.at[i] for i in range(2)], 64 * p, 16, s, ring_s)
            back_one = Gather(remote, 20, [pre.at[i] for i in range(2)], 0, 64, p, ring_p)
            row = 64 * p + 16 * s
            swap = remote(12, b["sent_y"], b["got_y"], across)

            def begin():
                load(k)
                for i in range(2):
                    part[i] = dot(qs[k], fac[k, pl.ds(col + i * h, h), :])
                one.first()

            def third():
                two.last()
                for i in range(2):
                    put(b["sent_y"].at[i], halves[i], row, 16)
                swap.start()

            def fourth():
                swap.wait()
                rows = pl.ds(aligned(row), 16)
                for i in range(2):
                    pre[i, rows, :] = ((part[i, rows, :] + decode(b["got_y"][i])) * (1.0 / SCALE)).astype(BF16)
                back_two.first()

            return [
                [begin], [one.second], [one.last, two.first], [two.second], [third], [fourth],
                [back_two.second], [back_two.last, back_one.first], [back_one.second],
                [back_one.last, lambda: finish(u)],
            ]
        if kind == 1:
            one = Scatter(remote, 0, halves, *coded("second"), 0, 64, s, ring_s)
            two = Direct(remote, 6, halves, *coded("first"), 64 * s, 16, p, ring_p)
            back_two = DirectGather(remote, 9, pre.at[y], 64 * s, 16, p, ring_p)
            back_one = Gather(remote, 20, [pre.at[y, i] for i in range(2)], 0, 64, s, ring_s)
            row = 64 * s + 16 * p
            swap = remote(13, pre.at[y], pre.at[y], across)

            def store():
                rows = pl.ds(aligned(row), 16)
                for i in range(2):
                    pre[y, i, rows, :] = (part[i, rows, :] * (1.0 / SCALE)).astype(BF16)

            return [
                [lambda: send_rows(u)], [lambda: sum_rows(u), one.first], [one.second],
                [one.last, two.first], [two.last, store, back_two.first], [back_two.last, back_one.first],
                [back_one.second], [back_one.last, swap.start], [swap.wait, lambda: finish(u)],
            ]
        one = Scatter(remote, 0, halves, *coded("first"), 0, 64, p, ring_p)
        two = Scatter(remote, 6, halves, *coded("second"), 64 * p, 16, s, ring_s)
        back_two = Gather(remote, 14, [pre.at[i] for i in range(2)], 64 * p, 16, s, ring_s)
        back_one = Gather(remote, 20, [pre.at[i] for i in range(2)], 0, 64, p, ring_p)
        rows = pl.ds(aligned(64 * p + 16 * s), 16)
        swap = remote(13, pre.at[y, rows, :], pre.at[y, rows, :], across)

        def store():
            for i in range(2):
                pre[y, rows, pl.ds(i * q, q)] = (part[i, rows, :] * (1.0 / SCALE)).astype(BF16)

        return [
            [lambda: send_rows(u)], [lambda: sum_rows(u), one.first], [one.second], [one.last, two.first],
            [two.second], [two.last, store, swap.start], [swap.wait, back_two.first], [back_two.second],
            [back_two.last, back_one.first], [back_one.second], [back_one.last, lambda: finish(u)],
        ]

    steps = [steps_of(u) for u in range(len(UNITS))]
    pl.semaphore_wait(barrier, len(everyone))
    for u in ORDER:
        for act in steps[u].pop(0):
            act()

    def fin_copy(d):
        who = (lay + d) % 4
        src = fin.at[pl.ds(pl.multiple_of(8 * who, 8), 8), :]
        return Remote(log, (fin_send, fin_recv), d - 1, src, rfin.at[d - 1], (who, tok))

    for d in (2, 3, 1):
        fin_copy(d).start()
    for c in log:
        c.wait_send()
    total = fin[pl.ds(pl.multiple_of(8 * lay, 8), 8), :]
    for d in (1, 2, 3):
        fin_copy(d).wait()
        total = total + rfin[d - 1]
    out_ref[...] = total


def local(inputs, out_grads, a_inverse, g_inverse, query_in, query_out):
    layers, tokens, width = inputs.shape
    depth = a_inverse.shape[2]
    rows = query_in.shape[1] * query_in.shape[2]
    dma = pltpu.SemaphoreType.DMA
    vmem = pltpu.VMEM
    scratch = [
        vmem((SLABS, rows, depth), BF16), vmem((SLABS, rows, depth), BF16),
        vmem((SLABS, width, depth), BF16), vmem((2, tokens, width), BF16),
        vmem((2, tokens, rows), F32), vmem((32, tokens), F32), vmem((3, 8, tokens), F32),
        dma((SLABS,)), dma((SLABS,)), dma((SLABS,)), dma((SLABS,)), dma((3,)), dma((3,)),
    ]
    for _, kind, _, w in UNITS:
        for shape, dtype in unit_scratch(kind, w).values():
            scratch.append(dma(shape) if dtype is None else vmem(shape, dtype))
    hbm = pl.BlockSpec(memory_space=pl.ANY)
    near = pl.BlockSpec(memory_space=pltpu.VMEM)
    scores = pl.pallas_call(
        kernel,
        out_shape=jax.ShapeDtypeStruct((8, tokens), F32),
        in_specs=[near, near, hbm, hbm, hbm, hbm],
        out_specs=near,
        scratch_shapes=scratch,
        compiler_params=pltpu.CompilerParams(
            collective_id=1, has_side_effects=True, vmem_limit_bytes=60 * 2**20
        ),
        cost_estimate=pl.CostEstimate(flops=6 * 10**9, bytes_accessed=26 * 10**6, transcendentals=0),
        name="influence",
    )(
        query_in.reshape(layers, rows, depth), query_out.reshape(layers, rows, depth),
        a_inverse, g_inverse, inputs, out_grads,
    )
    return scores.T


def solution(mesh):
    in_specs = (
        P("layer", "tok", None),
        P("layer", "tok", None),
        P("layer", None, "tok"),
        P("layer", None, "tok"),
        P("layer", None, None, "tok"),
        P("layer", None, None, "tok"),
    )
    return jax.shard_map(
        local, mesh=mesh, in_specs=in_specs, out_specs=P("tok", "layer"), check_vma=False
    )
```

```python
import jax
import jax.numpy as jnp
from jax import lax
from jax.experimental import pallas as pl
from jax.experimental.pallas import tpu as pltpu
from jax.sharding import PartitionSpec as P

MESH = pl.DeviceIdType.MESH
BF16, F32 = jnp.bfloat16, jnp.float32
SCALE = 2.0**29
NT = (((1,), (1,)), ((), ()))
SLABS = 4
WEST, EAST = 3, 1

UNITS = (
    (0, 0, 0, 2048, 0),
    (0, 1, 2048, 1024, 0),
    (0, 1, 3072, 1024, 0),
    (1, 0, 0, 3072, 0),
    (1, 1, 3072, 1024, 0),
    (2, 0, 0, 512, 0),
    (2, 2, 512, 2048, 0),
    (2, 1, 2560, 1536, 0),
    (3, 0, 0, 3072, 0),
    (3, 1, 3072, 1024, 0),
)

ORDER = (
    1, 0, 3, 4, 0, 6, 1, 7, 2, 8, 1, 9, 4, 0, 1, 4, 3, 8, 6, 0, 5, 0, 4, 3, 1, 7, 6, 8, 5, 3,
    2, 4, 7, 1, 8, 6, 9, 5, 3, 0, 2, 1, 7, 8, 6, 4, 9, 5, 0, 3, 2, 1, 7, 4, 6, 8, 9, 3, 5, 0,
    7, 9, 4, 2, 8, 3, 7, 6, 1, 2, 8, 7, 9, 0, 5, 2, 6, 9, 2, 5, 9, 6, 3, 0, 5, 4, 8, 2, 7, 6,
    3, 5, 8, 9, 6, 5,
)


def encode(v):
    a = v * jnp.abs(v)
    return (a * jnp.abs(a)).astype(BF16)


def decode(code):
    w = code.astype(F32)
    r = lax.rsqrt(jnp.maximum(jnp.abs(w), 1e-37))
    return w * (r * r * lax.rsqrt(r))


def aligned(row):
    return row if isinstance(row, int) else pl.multiple_of(row, 16)


class Remote:
    def __init__(self, log, sems, n, src, dst, who):
        self.log = log
        self.copy = pltpu.make_async_remote_copy(
            src_ref=src, dst_ref=dst, send_sem=sems[0].at[n], recv_sem=sems[1].at[n],
            device_id=who, device_id_type=MESH,
        )

    def start(self):
        self.copy.start()
        self.log.append(self.copy)

    def wait(self):
        self.copy.wait_recv()


def rows_loop(n, body):
    if n == 16:
        body(0)
    else:
        pl.loop(0, n // 16)(lambda i: body(pl.multiple_of(i * 16, 16)))


def put(dst, src, row0, n, more=None):
    def body(r):
        v = src[pl.ds(aligned(row0 + r), 16), :]
        if more is not None:
            v = v + decode(more[pl.ds(r, 16), :])
        dst[pl.ds(r, 16), :] = encode(v)

    rows_loop(n, body)


def add(src, row0, n, *coded):
    def body(r):
        rows = pl.ds(aligned(row0 + r), 16)
        v = src[rows, :]
        for c in coded:
            v = v + decode(c[pl.ds(r, 16), :])
        src[rows, :] = v

    rows_loop(n, body)


class Scatter:
    def __init__(self, remote, base, halves, sent, got, row0, n, me, ring):
        self.__dict__.update(locals())

    def copy(self, m):
        return self.remote(self.base + m, self.sent.at[m], self.got.at[m], self.ring[EAST if m % 2 == 0 else WEST])

    def row(self, d):
        return self.row0 + (self.me + d) % 4 * self.n

    def first(self):
        lo, hi = self.halves
        for m, (src, d) in enumerate(((hi, 2), (lo, 2), (lo, 1), (hi, 3))):
            put(self.sent.at[m], src, self.row(d), self.n)
            self.copy(m).start()

    def second(self):
        lo, hi = self.halves
        for m, (src, d) in enumerate(((hi, 1), (lo, 3))):
            self.copy(m).wait()
            put(self.sent.at[4 + m], src, self.row(d), self.n, self.got.at[m])
            self.copy(4 + m).start()

    def last(self):
        lo, hi = self.halves
        for m in (2, 3, 4, 5):
            self.copy(m).wait()
        add(lo, self.row(0), self.n, self.got.at[2], self.got.at[5])
        add(hi, self.row(0), self.n, self.got.at[3], self.got.at[4])


class Gather:
    def __init__(self, remote, base, halves, row0, n, me, ring):
        self.__dict__.update(locals())

    def copy(self, m):
        half = self.halves[(1, 0, 0, 1, 1, 0)[m]]
        d = (0, 0, 0, 0, 3, 1)[m]
        ref = half.at[pl.ds(aligned(self.row0 + (self.me + d) % 4 * self.n), self.n), :]
        return self.remote(self.base + m, ref, ref, self.ring[EAST if m % 2 == 0 else WEST])

    def first(self):
        for m in range(4):
            self.copy(m).start()

    def second(self):
        for m in range(2):
            self.copy(m).wait()
            self.copy(4 + m).start()

    def last(self):
        for m in (2, 3, 4, 5):
            self.copy(m).wait()


class Direct:
    second = None

    def __init__(self, remote, base, halves, sent, got, row0, n, me, ring):
        self.__dict__.update(locals())

    def copy(self, m):
        return self.remote(self.base + m, self.sent.at[m], self.got.at[m], self.ring[(2, 1, 3)[m]])

    def first(self):
        for m, d in enumerate((2, 1, 3)):
            for h in range(2):
                put(self.sent.at[m, h], self.halves[h], self.row0 + (self.me + d) % 4 * self.n, self.n)
            self.copy(m).start()

    def last(self):
        for m in range(3):
            self.copy(m).wait()
        for h in range(2):
            add(self.halves[h], self.row0 + self.me * self.n, self.n, *[self.got.at[m, h] for m in range(3)])


class DirectGather:
    second = None

    def __init__(self, remote, base, both, row0, n, me, ring):
        self.__dict__.update(locals())

    def copy(self, m):
        ref = self.both.at[:, pl.ds(aligned(self.row0 + self.me * self.n), self.n), :]
        return self.remote(self.base + m, ref, ref, self.ring[(2, 1, 3)[m]])

    def first(self):
        for m in range(3):
            self.copy(m).start()

    def last(self):
        for m in range(3):
            self.copy(m).wait()


def unit_scratch(kind, w, straight):
    h, q = w // 2, w // 4
    if kind == 0:
        got = dict(first=(6, 64, h), second=(3, 2, 16, h) if straight & 2 else (6, 16, h), y=(2, 16, h))
        own = dict(part=((2, 256, h), F32), pre=((2, 256, h), BF16))
    elif kind == 1:
        got = dict(first=(3, 2, 16, q), second=(6, 64, q))
        own = dict(part=((2, 256, q), F32), pre=((2, 2, 256, q), BF16), rows=((h, 128), BF16))
    else:
        got = dict(first=(6, 64, q), second=(3, 2, 16, q) if straight & 2 else (6, 16, q))
        own = dict(part=((2, 256, q), F32), pre=((2, 256, h), BF16), rows=((h, 128), BF16))
    for name, shape in got.items():
        own["sent_" + name] = (shape, BF16)
        own["got_" + name] = (shape, BF16)
    own["send_sem"] = own["recv_sem"] = ((26,), None)
    return own


def kernel(qi_ref, qo_ref, a_hbm, g_hbm, x_hbm, o_hbm, out_ref, *scratch):
    (qs, qx, fac, inp, side, fin, rfin, fac_sem, inp_sem, q_send, q_recv, fin_send, fin_recv) = scratch[:13]
    rest = list(scratch[13:])
    bufs = [{name: rest.pop(0) for name in unit_scratch(kind, w, straight)} for _, kind, _, w, straight in UNITS]

    lay, tok = lax.axis_index("layer"), lax.axis_index("tok")
    core = lay % 2
    y = tok // 16
    step_p, step_s = 1 + 3 * core, 4 - 3 * core
    p, s = (tok // step_p) % 4, (tok // step_s) % 4

    def at(p_, s_, y_):
        return (lay, y_ * 16 + p_ * step_p + s_ * step_s)

    ring_p = [None] + [at((p + d) % 4, s, y) for d in (1, 2, 3)]
    ring_s = [None] + [at(p, (s + d) % 4, y) for d in (1, 2, 3)]
    across = at(p, s, 1 - y)
    peers = [((lay + d) % 4, tok) for d in (1, 2, 3)]

    def fac_copy(k):
        return pltpu.make_async_copy((a_hbm, g_hbm)[k % 2].at[k // 2], fac.at[k], fac_sem.at[k])

    def inp_copy(k):
        return pltpu.make_async_copy((x_hbm, o_hbm)[k % 2].at[k // 2], inp.at[k % 2], inp_sem.at[k])

    barrier = pltpu.get_barrier_semaphore()
    everyone = [*ring_p[1:], *ring_s[1:], across, *peers]
    for who in everyone:
        pl.semaphore_signal(barrier, inc=1, device_id=who, device_id_type=MESH)
    for k in range(SLABS):
        fac_copy(k).start()
    for k in range(2):
        inp_copy(k).start()
    for k in range(SLABS):
        qs[k] = (qi_ref, qo_ref)[k % 2][k // 2] * jnp.asarray(SCALE, BF16)

    log = []
    loaded, asked, arrived = set(), set(), set()

    def load(k):
        if k not in loaded:
            loaded.add(k)
            fac_copy(k).wait()

    def q_copy(k):
        return Remote(log, (q_send, q_recv), k, qs.at[k], qx.at[k], across)

    def dot(a, b):
        return lax.dot_general(a, b, NT, preferred_element_type=F32)

    waiting, scored = [], []

    def finish(u):
        waiting.append(u)
        for v in sorted(waiting):
            k = UNITS[v][0]
            if all(w in scored for w, unit in enumerate(UNITS) if unit[0] < k // 2 * 2):
                waiting.remove(v)
                take(v, k)

    def take(u, k):
        _, kind, col, w, _ = UNITS[u]
        acc, data, pre = side.at[k % 2], inp.at[k % 2], bufs[u]["pre"]
        fresh = not any(UNITS[v][0] == k for v in scored)
        if fresh:
            inp_copy(k).wait()
        if kind == 1:
            pieces = [(pre[h // 2, h % 2], col + h * (w // 4), w // 4) for h in range(4)]
        else:
            pieces = [(pre[h], col + h * (w // 2), w // 2) for h in range(2)]
        for block, c, width in pieces:
            v = dot(data[:, pl.ds(c, width)], block)
            acc[...] = v if fresh else acc[...] + v
            fresh = False
        scored.append(u)
        if all(v in scored for v, unit in enumerate(UNITS) if unit[0] == k) and k + 2 < SLABS:
            inp_copy(k + 2).start()
        if all(v in scored for v, unit in enumerate(UNITS) if unit[0] // 2 == k // 2):
            layer_sum(k // 2)

    def layer_sum(layer):
        pick = jnp.where(
            lax.broadcasted_iota(jnp.int32, (32, 256), 1) // 8
            == lax.broadcasted_iota(jnp.int32, (32, 256), 0),
            1.0, 0.0,
        ).astype(BF16)
        for t in range(0, side.shape[1], 128):
            prod = side[0, pl.ds(t, 128), :] * side[1, pl.ds(t, 128), :]
            total = None
            for _ in range(3):
                top = prod.astype(BF16)
                prod = prod - top.astype(F32)
                part = dot(pick, top)
                total = part if total is None else total + part
            fin[:, pl.ds(t, 128)] = total if layer == 0 else fin[:, pl.ds(t, 128)] + total

    def exchange(u):
        k, _, col, w, _ = UNITS[u]
        h = w // 2
        src = (a_hbm, g_hbm)[k % 2].at[k // 2, pl.ds(aligned(col + (1 - y) * h), h), :]
        return Remote(log, (bufs[u]["send_sem"], bufs[u]["recv_sem"]), 12, src, bufs[u]["rows"], across)

    def send_rows(u):
        k = UNITS[u][0]
        if k not in asked:
            asked.add(k)
            q_copy(k).start()
        exchange(u).start()

    def sum_rows(u):
        k, _, col, w, _ = UNITS[u]
        load(k)
        if k not in arrived:
            arrived.add(k)
            q_copy(k).wait()
        exchange(u).wait()
        q, b = w // 4, bufs[u]
        for h in range(2):
            own = fac[k, pl.ds(aligned(col + y * (w // 2) + h * q), q), :]
            b["part"][h] = dot(qs[k], own) + dot(qx[k], b["rows"][pl.ds(h * q, q), :])

    def steps_of(u):
        k, kind, col, w, straight = UNITS[u]
        b = bufs[u]
        part, pre, h, q = b["part"], b["pre"], w // 2, w // 4

        def remote(n, src, dst, who):
            return Remote(log, (b["send_sem"], b["recv_sem"]), n, src, dst, who)

        halves = [part.at[i] for i in range(2)]
        def gather(direct, base, both, row0, n, me, ring):
            if direct:
                return DirectGather(remote, base, both, row0, n, me, ring)
            return Gather(remote, base, [both.at[i] for i in range(2)], row0, n, me, ring)

        coded = lambda name: (b["sent_" + name], b["got_" + name])
        if kind == 0:
            one = Scatter(remote, 0, halves, *coded("first"), 0, 64, p, ring_p)
            two = (Direct if straight & 2 else Scatter)(remote, 6, halves, *coded("second"), 64 * p, 16, s, ring_s)
            back_two = gather(straight & 2, 14, pre, 64 * p, 16, s, ring_s)
            back_one = gather(straight & 1, 20, pre, 0, 64, p, ring_p)
            row = 64 * p + 16 * s
            swap = remote(12, b["sent_y"], b["got_y"], across)

            def begin():
                load(k)
                for i in range(2):
                    part[i] = dot(qs[k], fac[k, pl.ds(col + i * h, h), :])
                one.first()

            def third():
                two.last()
                for i in range(2):
                    put(b["sent_y"].at[i], halves[i], row, 16)
                swap.start()

            def fourth():
                swap.wait()
                rows = pl.ds(aligned(row), 16)
                for i in range(2):
                    pre[i, rows, :] = ((part[i, rows, :] + decode(b["got_y"][i])) * (1.0 / SCALE)).astype(BF16)
                back_two.first()

            return [
                [begin], [one.second], [one.last, two.first], [two.second], [third], [fourth],
                [back_two.second], [back_two.last, back_one.first], [back_one.second],
                [back_one.last, lambda: finish(u)],
            ]
        if kind == 1:
            one = Scatter(remote, 0, halves, *coded("second"), 0, 64, s, ring_s)
            two = Direct(remote, 6, halves, *coded("first"), 64 * s, 16, p, ring_p)
            back_two = DirectGather(remote, 9, pre.at[y], 64 * s, 16, p, ring_p)
            back_one = gather(straight & 1, 20, pre.at[y], 0, 64, s, ring_s)
            row = 64 * s + 16 * p
            swap = remote(13, pre.at[y], pre.at[y], across)

            def store():
                rows = pl.ds(aligned(row), 16)
                for i in range(2):
                    pre[y, i, rows, :] = (part[i, rows, :] * (1.0 / SCALE)).astype(BF16)

            return [
                [lambda: send_rows(u)], [lambda: sum_rows(u), one.first], [one.second],
                [one.last, two.first], [two.last, store, back_two.first], [back_two.last, back_one.first],
                [back_one.second], [back_one.last, swap.start], [swap.wait, lambda: finish(u)],
            ]
        one = Scatter(remote, 0, halves, *coded("first"), 0, 64, p, ring_p)
        two = (Direct if straight & 2 else Scatter)(remote, 6, halves, *coded("second"), 64 * p, 16, s, ring_s)
        back_two = gather(straight & 2, 14, pre, 64 * p, 16, s, ring_s)
        back_one = gather(straight & 1, 20, pre, 0, 64, p, ring_p)
        rows = pl.ds(aligned(64 * p + 16 * s), 16)
        swap = remote(13, pre.at[y, rows, :], pre.at[y, rows, :], across)

        def store():
            for i in range(2):
                pre[y, rows, pl.ds(i * q, q)] = (part[i, rows, :] * (1.0 / SCALE)).astype(BF16)

        return [
            [lambda: send_rows(u)], [lambda: sum_rows(u), one.first], [one.second], [one.last, two.first],
            [two.second], [two.last, store, swap.start], [swap.wait, back_two.first], [back_two.second],
            [back_two.last, back_one.first], [back_one.second], [back_one.last, lambda: finish(u)],
        ]

    steps = [[acts for acts in steps_of(u) if acts != [None]] for u in range(len(UNITS))]
    pl.semaphore_wait(barrier, len(everyone))
    for u in ORDER:
        for act in steps[u].pop(0):
            act()

    def fin_copy(d):
        who = (lay + d) % 4
        src = fin.at[pl.ds(pl.multiple_of(8 * who, 8), 8), :]
        return Remote(log, (fin_send, fin_recv), d - 1, src, rfin.at[d - 1], (who, tok))

    for d in (2, 3, 1):
        fin_copy(d).start()
    for c in log:
        c.wait_send()
    total = fin[pl.ds(pl.multiple_of(8 * lay, 8), 8), :]
    for d in (1, 2, 3):
        fin_copy(d).wait()
        total = total + rfin[d - 1]
    out_ref[...] = total


def local(inputs, out_grads, a_inverse, g_inverse, query_in, query_out):
    layers, tokens, width = inputs.shape
    depth = a_inverse.shape[2]
    rows = query_in.shape[1] * query_in.shape[2]
    dma = pltpu.SemaphoreType.DMA
    vmem = pltpu.VMEM
    scratch = [
        vmem((SLABS, rows, depth), BF16), vmem((SLABS, rows, depth), BF16),
        vmem((SLABS, width, depth), BF16), vmem((2, tokens, width), BF16),
        vmem((2, tokens, rows), F32), vmem((32, tokens), F32), vmem((3, 8, tokens), F32),
        dma((SLABS,)), dma((SLABS,)), dma((SLABS,)), dma((SLABS,)), dma((3,)), dma((3,)),
    ]
    for _, kind, _, w, straight in UNITS:
        for shape, dtype in unit_scratch(kind, w, straight).values():
            scratch.append(dma(shape) if dtype is None else vmem(shape, dtype))
    hbm = pl.BlockSpec(memory_space=pl.ANY)
    near = pl.BlockSpec(memory_space=pltpu.VMEM)
    scores = pl.pallas_call(
        kernel,
        out_shape=jax.ShapeDtypeStruct((8, tokens), F32),
        in_specs=[near, near, hbm, hbm, hbm, hbm],
        out_specs=near,
        scratch_shapes=scratch,
        compiler_params=pltpu.CompilerParams(
            collective_id=1, has_side_effects=True, vmem_limit_bytes=60 * 2**20
        ),
        cost_estimate=pl.CostEstimate(flops=6 * 10**9, bytes_accessed=26 * 10**6, transcendentals=0),
        name="influence",
    )(
        query_in.reshape(layers, rows, depth), query_out.reshape(layers, rows, depth),
        a_inverse, g_inverse, inputs, out_grads,
    )
    return scores.T


def solution(mesh):
    in_specs = (
        P("layer", "tok", None),
        P("layer", "tok", None),
        P("layer", None, "tok"),
        P("layer", None, "tok"),
        P("layer", None, None, "tok"),
        P("layer", None, None, "tok"),
    )
    return jax.shard_map(
        local, mesh=mesh, in_specs=in_specs, out_specs=P("tok", "layer"), check_vma=False
    )
```

```python
import jax
import jax.numpy as jnp
from jax import lax
from jax.experimental import pallas as pl
from jax.experimental.pallas import tpu as pltpu
from jax.sharding import PartitionSpec as P

MESH = pl.DeviceIdType.MESH
BF16, F32 = jnp.bfloat16, jnp.float32
SCALE = 2.0**29
NT = (((1,), (1,)), ((), ()))
SLABS = 4
LATE = 10
WEST, EAST = 3, 1

UNITS = (
    (0, 0, 0, 2048, 0),
    (0, 1, 2048, 2048, 0),
    (1, 0, 0, 3072, 0),
    (1, 1, 3072, 1024, 0),
    (2, 0, 0, 512, 0),
    (2, 2, 512, 2048, 0),
    (2, 1, 2560, 1536, 0),
    (3, 0, 0, 3072, 0),
    (3, 1, 3072, 1024, 1),
)

ORDER = (
    4, 0, 1, 3, 5, 2, 6, 7, 0, 1, 2, 4, 7, 3, 1, 3, 8, 0, 1, 5, 4, 2, 0, 3, 4, 7, 6, 1, 5, 2,
    0, 7, 8, 3, 1, 6, 4, 5, 0, 2, 8, 7, 1, 3, 6, 5, 0, 2, 4, 1, 8, 3, 7, 5, 6, 2, 0, 4, 8, 3,
    7, 6, 2, 0, 4, 7, 6, 8, 2, 1, 5, 6, 8, 5, 4, 5, 7, 3, 0, 2, 5, 4, 6, 7, 8, 5,
)


def encode(v):
    a = v * jnp.abs(v)
    return (a * jnp.abs(a)).astype(BF16)


def decode(code):
    w = code.astype(F32)
    r = lax.rsqrt(jnp.maximum(jnp.abs(w), 1e-37))
    return w * (r * r * lax.rsqrt(r))


def aligned(row):
    return row if isinstance(row, int) else pl.multiple_of(row, 16)


class Remote:
    def __init__(self, log, sems, n, src, dst, who):
        self.log = log
        self.copy = pltpu.make_async_remote_copy(
            src_ref=src, dst_ref=dst, send_sem=sems[0].at[n], recv_sem=sems[1].at[n],
            device_id=who, device_id_type=MESH,
        )

    def start(self):
        self.copy.start()
        self.log.append(self.copy)

    def wait(self):
        self.copy.wait_recv()


def rows_loop(n, body):
    if n == 16:
        body(0)
    else:
        pl.loop(0, n // 16)(lambda i: body(pl.multiple_of(i * 16, 16)))


def put(dst, src, row0, n, more=None):
    def body(r):
        v = src[pl.ds(aligned(row0 + r), 16), :]
        if more is not None:
            v = v + decode(more[pl.ds(r, 16), :])
        dst[pl.ds(r, 16), :] = encode(v)

    rows_loop(n, body)


def add(src, row0, n, *coded):
    def body(r):
        rows = pl.ds(aligned(row0 + r), 16)
        v = src[rows, :]
        for c in coded:
            v = v + decode(c[pl.ds(r, 16), :])
        src[rows, :] = v

    rows_loop(n, body)


class Scatter:
    def __init__(self, remote, base, halves, sent, got, row0, n, me, ring):
        self.__dict__.update(locals())

    def copy(self, m):
        return self.remote(self.base + m, self.sent.at[m], self.got.at[m], self.ring[EAST if m % 2 == 0 else WEST])

    def row(self, d):
        return self.row0 + (self.me + d) % 4 * self.n

    def first(self):
        lo, hi = self.halves
        for m, (src, d) in enumerate(((hi, 2), (lo, 2), (lo, 1), (hi, 3))):
            put(self.sent.at[m], src, self.row(d), self.n)
            self.copy(m).start()

    def second(self):
        lo, hi = self.halves
        for m, (src, d) in enumerate(((hi, 1), (lo, 3))):
            self.copy(m).wait()
            put(self.sent.at[4 + m], src, self.row(d), self.n, self.got.at[m])
            self.copy(4 + m).start()

    def last(self):
        lo, hi = self.halves
        for m in (2, 3, 4, 5):
            self.copy(m).wait()
        add(lo, self.row(0), self.n, self.got.at[2], self.got.at[5])
        add(hi, self.row(0), self.n, self.got.at[3], self.got.at[4])


class Gather:
    def __init__(self, remote, base, halves, row0, n, me, ring):
        self.__dict__.update(locals())

    def copy(self, m):
        half = self.halves[(1, 0, 0, 1, 1, 0)[m]]
        d = (0, 0, 0, 0, 3, 1)[m]
        ref = half.at[pl.ds(aligned(self.row0 + (self.me + d) % 4 * self.n), self.n), :]
        return self.remote(self.base + m, ref, ref, self.ring[EAST if m % 2 == 0 else WEST])

    def first(self):
        for m in range(4):
            self.copy(m).start()

    def second(self):
        for m in range(2):
            self.copy(m).wait()
            self.copy(4 + m).start()

    def last(self):
        for m in (2, 3, 4, 5):
            self.copy(m).wait()


class Direct:
    second = None

    def __init__(self, remote, base, halves, sent, got, row0, n, me, ring):
        self.__dict__.update(locals())

    def copy(self, m):
        return self.remote(self.base + m, self.sent.at[m], self.got.at[m], self.ring[(2, 1, 3)[m]])

    def first(self):
        for m, d in enumerate((2, 1, 3)):
            for h in range(2):
                put(self.sent.at[m, h], self.halves[h], self.row0 + (self.me + d) % 4 * self.n, self.n)
            self.copy(m).start()

    def last(self):
        for m in range(3):
            self.copy(m).wait()
        for h in range(2):
            add(self.halves[h], self.row0 + self.me * self.n, self.n, *[self.got.at[m, h] for m in range(3)])


class DirectGather:
    second = None

    def __init__(self, remote, base, both, row0, n, me, ring):
        self.__dict__.update(locals())

    def copy(self, m):
        ref = self.both.at[:, pl.ds(aligned(self.row0 + self.me * self.n), self.n), :]
        return self.remote(self.base + m, ref, ref, self.ring[(2, 1, 3)[m]])

    def first(self):
        for m in range(3):
            self.copy(m).start()

    def last(self):
        for m in range(3):
            self.copy(m).wait()


def unit_scratch(kind, w, straight):
    h, q = w // 2, w // 4
    if kind == 0:
        got = dict(first=(6, 64, h), second=(3, 2, 16, h) if straight & 2 else (6, 16, h), y=(2, 16, h))
        own = dict(part=((2, 256, h), F32), pre=((2, 256, h), BF16))
    elif kind == 1:
        got = dict(first=(3, 2, 16, q), second=(6, 64, q))
        own = dict(part=((2, 256, q), F32), pre=((2, 2, 256, q), BF16), rows=((h, 128), BF16))
    else:
        got = dict(first=(6, 64, q), second=(3, 2, 16, q) if straight & 2 else (6, 16, q))
        own = dict(part=((2, 256, q), F32), pre=((2, 256, h), BF16), rows=((h, 128), BF16))
    for name, shape in got.items():
        own["sent_" + name] = (shape, BF16)
        own["got_" + name] = (shape, BF16)
    own["send_sem"] = own["recv_sem"] = ((26,), None)
    return own


def kernel(qi_ref, qo_ref, a_hbm, g_hbm, x_hbm, o_hbm, out_ref, *scratch):
    (qs, qx, fac, inp, side, fin, rfin, fac_sem, inp_sem, q_send, q_recv, fin_send, fin_recv) = scratch[:13]
    rest = list(scratch[13:])
    bufs = [{name: rest.pop(0) for name in unit_scratch(kind, w, straight)} for _, kind, _, w, straight in UNITS]

    lay, tok = lax.axis_index("layer"), lax.axis_index("tok")
    core = lay % 2
    y = tok // 16
    step_p, step_s = 1 + 3 * core, 4 - 3 * core
    p, s = (tok // step_p) % 4, (tok // step_s) % 4

    def at(p_, s_, y_):
        return (lay, y_ * 16 + p_ * step_p + s_ * step_s)

    ring_p = [None] + [at((p + d) % 4, s, y) for d in (1, 2, 3)]
    ring_s = [None] + [at(p, (s + d) % 4, y) for d in (1, 2, 3)]
    across = at(p, s, 1 - y)
    peers = [((lay + d) % 4, tok) for d in (1, 2, 3)]

    def fac_copy(k):
        return pltpu.make_async_copy((a_hbm, g_hbm)[k % 2].at[k // 2], fac.at[k], fac_sem.at[k])

    def inp_copy(k):
        return pltpu.make_async_copy((x_hbm, o_hbm)[k % 2].at[k // 2], inp.at[k % 2], inp_sem.at[k])

    barrier = pltpu.get_barrier_semaphore()
    everyone = [*ring_p[1:], *ring_s[1:], across, *peers]
    for who in everyone:
        pl.semaphore_signal(barrier, inc=1, device_id=who, device_id_type=MESH)
    for k in range(SLABS):
        fac_copy(k).start()
    for k in range(SLABS):
        qs[k] = (qi_ref, qo_ref)[k % 2][k // 2] * jnp.asarray(SCALE, BF16)

    log = []
    loaded, asked, arrived = set(), set(), set()

    def load(k):
        if k not in loaded:
            loaded.add(k)
            fac_copy(k).wait()

    def q_copy(k):
        return Remote(log, (q_send, q_recv), k, qs.at[k], qx.at[k], across)

    def dot(a, b):
        return lax.dot_general(a, b, NT, preferred_element_type=F32)

    waiting, scored = [], []

    def finish(u):
        waiting.append(u)
        for v in sorted(waiting):
            k = UNITS[v][0]
            if all(w in scored for w, unit in enumerate(UNITS) if unit[0] < k // 2 * 2):
                waiting.remove(v)
                take(v, k)

    def take(u, k):
        _, kind, col, w, _ = UNITS[u]
        acc, data, pre = side.at[k % 2], inp.at[k % 2], bufs[u]["pre"]
        fresh = not any(UNITS[v][0] == k for v in scored)
        if fresh:
            inp_copy(k).wait()
        if kind == 1:
            pieces = [(pre[h // 2, h % 2], col + h * (w // 4), w // 4) for h in range(4)]
        else:
            pieces = [(pre[h], col + h * (w // 2), w // 2) for h in range(2)]
        for block, c, width in pieces:
            v = dot(data[:, pl.ds(c, width)], block)
            acc[...] = v if fresh else acc[...] + v
            fresh = False
        scored.append(u)
        if all(v in scored for v, unit in enumerate(UNITS) if unit[0] == k) and k + 2 < SLABS:
            inp_copy(k + 2).start()
        if all(v in scored for v, unit in enumerate(UNITS) if unit[0] // 2 == k // 2):
            layer_sum(k // 2)

    def layer_sum(layer):
        pick = jnp.where(
            lax.broadcasted_iota(jnp.int32, (32, 256), 1) // 8
            == lax.broadcasted_iota(jnp.int32, (32, 256), 0),
            1.0, 0.0,
        ).astype(BF16)
        for t in range(0, side.shape[1], 128):
            prod = side[0, pl.ds(t, 128), :] * side[1, pl.ds(t, 128), :]
            total = None
            for _ in range(3):
                top = prod.astype(BF16)
                prod = prod - top.astype(F32)
                part = dot(pick, top)
                total = part if total is None else total + part
            fin[:, pl.ds(t, 128)] = total if layer == 0 else fin[:, pl.ds(t, 128)] + total

    def exchange(u):
        k, _, col, w, _ = UNITS[u]
        h = w // 2
        src = (a_hbm, g_hbm)[k % 2].at[k // 2, pl.ds(aligned(col + (1 - y) * h), h), :]
        return Remote(log, (bufs[u]["send_sem"], bufs[u]["recv_sem"]), 12, src, bufs[u]["rows"], across)

    def send_rows(u):
        k = UNITS[u][0]
        if k not in asked:
            asked.add(k)
            q_copy(k).start()
        exchange(u).start()

    def sum_rows(u):
        k, _, col, w, _ = UNITS[u]
        load(k)
        if k not in arrived:
            arrived.add(k)
            q_copy(k).wait()
        exchange(u).wait()
        q, b = w // 4, bufs[u]
        for h in range(2):
            own = fac[k, pl.ds(aligned(col + y * (w // 2) + h * q), q), :]
            b["part"][h] = dot(qs[k], own) + dot(qx[k], b["rows"][pl.ds(h * q, q), :])

    def steps_of(u):
        k, kind, col, w, straight = UNITS[u]
        b = bufs[u]
        part, pre, h, q = b["part"], b["pre"], w // 2, w // 4

        def remote(n, src, dst, who):
            return Remote(log, (b["send_sem"], b["recv_sem"]), n, src, dst, who)

        halves = [part.at[i] for i in range(2)]
        def gather(direct, base, both, row0, n, me, ring):
            if direct:
                return DirectGather(remote, base, both, row0, n, me, ring)
            return Gather(remote, base, [both.at[i] for i in range(2)], row0, n, me, ring)

        coded = lambda name: (b["sent_" + name], b["got_" + name])
        if kind == 0:
            one = Scatter(remote, 0, halves, *coded("first"), 0, 64, p, ring_p)
            two = (Direct if straight & 2 else Scatter)(remote, 6, halves, *coded("second"), 64 * p, 16, s, ring_s)
            back_two = gather(straight & 2, 14, pre, 64 * p, 16, s, ring_s)
            back_one = gather(straight & 1, 20, pre, 0, 64, p, ring_p)
            row = 64 * p + 16 * s
            swap = remote(12, b["sent_y"], b["got_y"], across)

            def begin():
                load(k)
                for i in range(2):
                    part[i] = dot(qs[k], fac[k, pl.ds(col + i * h, h), :])
                one.first()

            def third():
                two.last()
                for i in range(2):
                    put(b["sent_y"].at[i], halves[i], row, 16)
                swap.start()

            def fourth():
                swap.wait()
                rows = pl.ds(aligned(row), 16)
                for i in range(2):
                    pre[i, rows, :] = ((part[i, rows, :] + decode(b["got_y"][i])) * (1.0 / SCALE)).astype(BF16)
                back_two.first()

            return [
                [begin], [one.second], [one.last, two.first], [two.second], [third], [fourth],
                [back_two.second], [back_two.last, back_one.first], [back_one.second],
                [back_one.last, lambda: finish(u)],
            ]
        if kind == 1:
            one = Scatter(remote, 0, halves, *coded("second"), 0, 64, s, ring_s)
            two = Direct(remote, 6, halves, *coded("first"), 64 * s, 16, p, ring_p)
            back_two = DirectGather(remote, 9, pre.at[y], 64 * s, 16, p, ring_p)
            back_one = gather(straight & 1, 20, pre.at[y], 0, 64, s, ring_s)
            row = 64 * s + 16 * p
            swap = remote(13, pre.at[y], pre.at[y], across)

            def store():
                rows = pl.ds(aligned(row), 16)
                for i in range(2):
                    pre[y, i, rows, :] = (part[i, rows, :] * (1.0 / SCALE)).astype(BF16)

            return [
                [lambda: send_rows(u)], [lambda: sum_rows(u), one.first], [one.second],
                [one.last, two.first], [two.last, store, back_two.first], [back_two.last, back_one.first],
                [back_one.second], [back_one.last, swap.start], [swap.wait, lambda: finish(u)],
            ]
        one = Scatter(remote, 0, halves, *coded("first"), 0, 64, p, ring_p)
        two = (Direct if straight & 2 else Scatter)(remote, 6, halves, *coded("second"), 64 * p, 16, s, ring_s)
        back_two = gather(straight & 2, 14, pre, 64 * p, 16, s, ring_s)
        back_one = gather(straight & 1, 20, pre, 0, 64, p, ring_p)
        rows = pl.ds(aligned(64 * p + 16 * s), 16)
        swap = remote(13, pre.at[y, rows, :], pre.at[y, rows, :], across)

        def store():
            for i in range(2):
                pre[y, rows, pl.ds(i * q, q)] = (part[i, rows, :] * (1.0 / SCALE)).astype(BF16)

        return [
            [lambda: send_rows(u)], [lambda: sum_rows(u), one.first], [one.second], [one.last, two.first],
            [two.second], [two.last, store, swap.start], [swap.wait, back_two.first], [back_two.second],
            [back_two.last, back_one.first], [back_one.second], [back_one.last, lambda: finish(u)],
        ]

    steps = [[acts for acts in steps_of(u) if acts != [None]] for u in range(len(UNITS))]
    pl.semaphore_wait(barrier, len(everyone))
    for i, u in enumerate(ORDER):
        for act in steps[u].pop(0):
            act()
        if i in (LATE, LATE + 4):
            inp_copy((i - LATE) // 4).start()

    def fin_copy(d):
        who = (lay + d) % 4
        src = fin.at[pl.ds(pl.multiple_of(8 * who, 8), 8), :]
        return Remote(log, (fin_send, fin_recv), d - 1, src, rfin.at[d - 1], (who, tok))

    for d in (2, 3, 1):
        fin_copy(d).start()
    for c in log:
        c.wait_send()
    total = fin[pl.ds(pl.multiple_of(8 * lay, 8), 8), :]
    for d in (1, 2, 3):
        fin_copy(d).wait()
        total = total + rfin[d - 1]
    out_ref[...] = total


def local(inputs, out_grads, a_inverse, g_inverse, query_in, query_out):
    layers, tokens, width = inputs.shape
    depth = a_inverse.shape[2]
    rows = query_in.shape[1] * query_in.shape[2]
    dma = pltpu.SemaphoreType.DMA
    vmem = pltpu.VMEM
    scratch = [
        vmem((SLABS, rows, depth), BF16), vmem((SLABS, rows, depth), BF16),
        vmem((SLABS, width, depth), BF16), vmem((2, tokens, width), BF16),
        vmem((2, tokens, rows), F32), vmem((32, tokens), F32), vmem((3, 8, tokens), F32),
        dma((SLABS,)), dma((SLABS,)), dma((SLABS,)), dma((SLABS,)), dma((3,)), dma((3,)),
    ]
    for _, kind, _, w, straight in UNITS:
        for shape, dtype in unit_scratch(kind, w, straight).values():
            scratch.append(dma(shape) if dtype is None else vmem(shape, dtype))
    hbm = pl.BlockSpec(memory_space=pl.ANY)
    near = pl.BlockSpec(memory_space=pltpu.VMEM)
    scores = pl.pallas_call(
        kernel,
        out_shape=jax.ShapeDtypeStruct((8, tokens), F32),
        in_specs=[near, near, hbm, hbm, hbm, hbm],
        out_specs=near,
        scratch_shapes=scratch,
        compiler_params=pltpu.CompilerParams(
            collective_id=1, has_side_effects=True, vmem_limit_bytes=60 * 2**20
        ),
        cost_estimate=pl.CostEstimate(flops=6 * 10**9, bytes_accessed=26 * 10**6, transcendentals=0),
        name="influence",
    )(
        query_in.reshape(layers, rows, depth), query_out.reshape(layers, rows, depth),
        a_inverse, g_inverse, inputs, out_grads,
    )
    return scores.T


def solution(mesh):
    in_specs = (
        P("layer", "tok", None),
        P("layer", "tok", None),
        P("layer", None, "tok"),
        P("layer", None, "tok"),
        P("layer", None, None, "tok"),
        P("layer", None, None, "tok"),
    )
    return jax.shard_map(
        local, mesh=mesh, in_specs=in_specs, out_specs=P("tok", "layer"), check_vma=False
    )
```

```python
import jax
import jax.numpy as jnp
from jax import lax
from jax.experimental import pallas as pl
from jax.experimental.pallas import tpu as pltpu
from jax.sharding import PartitionSpec as P

MESH = pl.DeviceIdType.MESH
BF16, F32 = jnp.bfloat16, jnp.float32
SCALE = 2.0**29
NT = (((1,), (1,)), ((), ()))
SLABS = 4
LATE = 10
WEST, EAST = 3, 1

UNITS = (
    (0, 0, 0, 2048, 0),
    (0, 1, 2048, 2048, 0),
    (1, 0, 0, 3072, 0),
    (1, 1, 3072, 1024, 0),
    (2, 0, 0, 512, 0),
    (2, 2, 512, 2048, 0),
    (2, 1, 2560, 1536, 0),
    (3, 0, 0, 3072, 0),
    (3, 1, 3072, 1024, 1),
)

ORDER = (
    4, 0, 1, 3, 5, 2, 6, 7, 0, 1, 2, 4, 7, 3, 1, 3, 8, 0, 1, 5, 4, 2, 0, 3, 4, 7, 6, 1, 5, 2,
    0, 7, 8, 3, 1, 6, 4, 5, 0, 2, 8, 7, 1, 3, 6, 5, 0, 2, 4, 1, 8, 3, 7, 5, 6, 2, 0, 4, 8, 3,
    7, 6, 2, 0, 4, 7, 6, 8, 2, 1, 5, 6, 8, 5, 4, 5, 7, 3, 0, 2, 5, 4, 6, 7, 8, 5,
)


def encode(v):
    a = v * jnp.abs(v)
    return (a * jnp.abs(a)).astype(BF16)


def decode(code):
    w = code.astype(F32)
    r = lax.rsqrt(jnp.maximum(jnp.abs(w), 1e-37))
    return w * (r * r * lax.rsqrt(r))


def aligned(row):
    return row if isinstance(row, int) else pl.multiple_of(row, 16)


class Remote:
    def __init__(self, log, sems, n, src, dst, who):
        self.log = log
        self.copy = pltpu.make_async_remote_copy(
            src_ref=src, dst_ref=dst, send_sem=sems[0].at[n], recv_sem=sems[1].at[n],
            device_id=who, device_id_type=MESH,
        )

    def start(self):
        self.copy.start()
        self.log.append(self.copy)

    def wait(self):
        self.copy.wait_recv()


def rows_loop(n, body):
    if n == 16:
        body(0)
    else:
        pl.loop(0, n // 16)(lambda i: body(pl.multiple_of(i * 16, 16)))


def put(dst, src, row0, n, more=None):
    def body(r):
        v = src[pl.ds(aligned(row0 + r), 16), :]
        if more is not None:
            v = v + decode(more[pl.ds(r, 16), :])
        dst[pl.ds(r, 16), :] = encode(v)

    rows_loop(n, body)


def add(src, row0, n, *coded):
    def body(r):
        rows = pl.ds(aligned(row0 + r), 16)
        v = src[rows, :]
        for c in coded:
            v = v + decode(c[pl.ds(r, 16), :])
        src[rows, :] = v

    rows_loop(n, body)


class Scatter:
    def __init__(self, remote, base, halves, sent, got, row0, n, me, ring):
        self.__dict__.update(locals())

    def copy(self, m):
        return self.remote(self.base + m, self.sent.at[m], self.got.at[m], self.ring[EAST if m % 2 == 0 else WEST])

    def row(self, d):
        return self.row0 + (self.me + d) % 4 * self.n

    def first(self):
        lo, hi = self.halves
        for m, (src, d) in enumerate(((hi, 2), (lo, 2), (lo, 1), (hi, 3))):
            put(self.sent.at[m], src, self.row(d), self.n)
            self.copy(m).start()

    def second(self):
        lo, hi = self.halves
        for m, (src, d) in enumerate(((hi, 1), (lo, 3))):
            self.copy(m).wait()
            put(self.sent.at[4 + m], src, self.row(d), self.n, self.got.at[m])
            self.copy(4 + m).start()

    def last(self):
        lo, hi = self.halves
        for m in (2, 3, 4, 5):
            self.copy(m).wait()
        add(lo, self.row(0), self.n, self.got.at[2], self.got.at[5])
        add(hi, self.row(0), self.n, self.got.at[3], self.got.at[4])


class Gather:
    def __init__(self, remote, base, halves, row0, n, me, ring):
        self.__dict__.update(locals())

    def copy(self, m):
        half = self.halves[(1, 0, 0, 1, 1, 0)[m]]
        d = (0, 0, 0, 0, 3, 1)[m]
        ref = half.at[pl.ds(aligned(self.row0 + (self.me + d) % 4 * self.n), self.n), :]
        return self.remote(self.base + m, ref, ref, self.ring[EAST if m % 2 == 0 else WEST])

    def first(self):
        for m in range(4):
            self.copy(m).start()

    def second(self):
        for m in range(2):
            self.copy(m).wait()
            self.copy(4 + m).start()

    def last(self):
        for m in (2, 3, 4, 5):
            self.copy(m).wait()


class Direct:
    second = None

    def __init__(self, remote, base, halves, sent, got, row0, n, me, ring):
        self.__dict__.update(locals())

    def copy(self, m):
        return self.remote(self.base + m, self.sent.at[m], self.got.at[m], self.ring[(2, 1, 3)[m]])

    def first(self):
        for m, d in enumerate((2, 1, 3)):
            for h in range(2):
                put(self.sent.at[m, h], self.halves[h], self.row0 + (self.me + d) % 4 * self.n, self.n)
            self.copy(m).start()

    def last(self):
        for m in range(3):
            self.copy(m).wait()
        for h in range(2):
            add(self.halves[h], self.row0 + self.me * self.n, self.n, *[self.got.at[m, h] for m in range(3)])


class DirectGather:
    second = None

    def __init__(self, remote, base, both, row0, n, me, ring):
        self.__dict__.update(locals())

    def copy(self, m):
        ref = self.both.at[:, pl.ds(aligned(self.row0 + self.me * self.n), self.n), :]
        return self.remote(self.base + m, ref, ref, self.ring[(2, 1, 3)[m]])

    def first(self):
        for m in range(3):
            self.copy(m).start()

    def last(self):
        for m in range(3):
            self.copy(m).wait()


def unit_scratch(kind, w, straight):
    h, q = w // 2, w // 4
    if kind == 0:
        got = dict(first=(6, 64, h), second=(3, 2, 16, h) if straight & 2 else (6, 16, h), y=(2, 16, h))
        own = dict(part=((2, 256, h), F32), pre=((2, 256, h), BF16))
    elif kind == 1:
        got = dict(first=(3, 2, 16, q), second=(6, 64, q))
        own = dict(part=((2, 256, q), F32), pre=((2, 2, 256, q), BF16), rows=((h, 128), BF16))
    else:
        got = dict(first=(6, 64, q), second=(3, 2, 16, q) if straight & 2 else (6, 16, q))
        own = dict(part=((2, 256, q), F32), pre=((2, 256, h), BF16), rows=((h, 128), BF16))
    for name, shape in got.items():
        own["sent_" + name] = (shape, BF16)
        own["got_" + name] = (shape, BF16)
    own["send_sem"] = own["recv_sem"] = ((26,), None)
    return own


def kernel(qi_ref, qo_ref, a_hbm, g_hbm, x_hbm, o_hbm, out_ref, *scratch):
    (qs, qx, fac, inp, side, fin, rfin, fac_sem, inp_sem, q_send, q_recv, fin_send, fin_recv) = scratch[:13]
    rest = list(scratch[13:])
    bufs = [{name: rest.pop(0) for name in unit_scratch(kind, w, straight)} for _, kind, _, w, straight in UNITS]

    lay, tok = lax.axis_index("layer"), lax.axis_index("tok")
    core = lay % 2
    y = tok // 16
    step_p, step_s = 1 + 3 * core, 4 - 3 * core
    p, s = (tok // step_p) % 4, (tok // step_s) % 4

    def at(p_, s_, y_):
        return (lay, y_ * 16 + p_ * step_p + s_ * step_s)

    ring_p = [None] + [at((p + d) % 4, s, y) for d in (1, 2, 3)]
    ring_s = [None] + [at(p, (s + d) % 4, y) for d in (1, 2, 3)]
    across = at(p, s, 1 - y)
    peers = [((lay + d) % 4, tok) for d in (1, 2, 3)]

    def fac_copy(k):
        return pltpu.make_async_copy((a_hbm, g_hbm)[k % 2].at[k // 2], fac.at[k], fac_sem.at[k])

    def inp_copy(k):
        return pltpu.make_async_copy((x_hbm, o_hbm)[k % 2].at[k // 2], inp.at[k % 2], inp_sem.at[k])

    fac_copy(0).start()
    barrier = pltpu.get_barrier_semaphore()
    everyone = [*ring_p[1:], *ring_s[1:], across, *peers]
    for who in everyone:
        pl.semaphore_signal(barrier, inc=1, device_id=who, device_id_type=MESH)
    for k in range(SLABS):
        qs[k] = (qi_ref, qo_ref)[k % 2][k // 2] * jnp.asarray(SCALE, BF16)

    for k in range(1, SLABS):
        fac_copy(k).start()
    log = []
    loaded, asked, arrived = set(), set(), set()

    def load(k):
        if k not in loaded:
            loaded.add(k)
            fac_copy(k).wait()

    def q_copy(k):
        return Remote(log, (q_send, q_recv), k, qs.at[k], qx.at[k], across)

    def dot(a, b):
        return lax.dot_general(a, b, NT, preferred_element_type=F32)

    waiting, scored = [], []

    def finish(u):
        waiting.append(u)
        for v in sorted(waiting):
            k = UNITS[v][0]
            if all(w in scored for w, unit in enumerate(UNITS) if unit[0] < k // 2 * 2):
                waiting.remove(v)
                take(v, k)

    def take(u, k):
        _, kind, col, w, _ = UNITS[u]
        acc, data, pre = side.at[k % 2], inp.at[k % 2], bufs[u]["pre"]
        fresh = not any(UNITS[v][0] == k for v in scored)
        if fresh:
            inp_copy(k).wait()
        if kind == 1:
            pieces = [(pre[h // 2, h % 2], col + h * (w // 4), w // 4) for h in range(4)]
        else:
            pieces = [(pre[h], col + h * (w // 2), w // 2) for h in range(2)]
        for block, c, width in pieces:
            v = dot(data[:, pl.ds(c, width)], block)
            acc[...] = v if fresh else acc[...] + v
            fresh = False
        scored.append(u)
        if all(v in scored for v, unit in enumerate(UNITS) if unit[0] == k) and k + 2 < SLABS:
            inp_copy(k + 2).start()
        if all(v in scored for v, unit in enumerate(UNITS) if unit[0] // 2 == k // 2):
            layer_sum(k // 2)

    def layer_sum(layer):
        pick = jnp.where(
            lax.broadcasted_iota(jnp.int32, (32, 256), 1) // 8
            == lax.broadcasted_iota(jnp.int32, (32, 256), 0),
            1.0, 0.0,
        ).astype(BF16)
        for t in range(0, side.shape[1], 128):
            prod = side[0, pl.ds(t, 128), :] * side[1, pl.ds(t, 128), :]
            total = None
            for _ in range(3):
                top = prod.astype(BF16)
                prod = prod - top.astype(F32)
                part = dot(pick, top)
                total = part if total is None else total + part
            fin[:, pl.ds(t, 128)] = total if layer == 0 else fin[:, pl.ds(t, 128)] + total

    def exchange(u):
        k, _, col, w, _ = UNITS[u]
        h = w // 2
        src = (a_hbm, g_hbm)[k % 2].at[k // 2, pl.ds(aligned(col + (1 - y) * h), h), :]
        return Remote(log, (bufs[u]["send_sem"], bufs[u]["recv_sem"]), 12, src, bufs[u]["rows"], across)

    def send_rows(u):
        k = UNITS[u][0]
        if k not in asked:
            asked.add(k)
            q_copy(k).start()
        exchange(u).start()

    def sum_rows(u):
        k, _, col, w, _ = UNITS[u]
        load(k)
        if k not in arrived:
            arrived.add(k)
            q_copy(k).wait()
        exchange(u).wait()
        q, b = w // 4, bufs[u]
        for h in range(2):
            own = fac[k, pl.ds(aligned(col + y * (w // 2) + h * q), q), :]
            b["part"][h] = dot(qs[k], own) + dot(qx[k], b["rows"][pl.ds(h * q, q), :])

    def steps_of(u):
        k, kind, col, w, straight = UNITS[u]
        b = bufs[u]
        part, pre, h, q = b["part"], b["pre"], w // 2, w // 4

        def remote(n, src, dst, who):
            return Remote(log, (b["send_sem"], b["recv_sem"]), n, src, dst, who)

        halves = [part.at[i] for i in range(2)]
        def gather(direct, base, both, row0, n, me, ring):
            if direct:
                return DirectGather(remote, base, both, row0, n, me, ring)
            return Gather(remote, base, [both.at[i] for i in range(2)], row0, n, me, ring)

        coded = lambda name: (b["sent_" + name], b["got_" + name])
        if kind == 0:
            one = Scatter(remote, 0, halves, *coded("first"), 0, 64, p, ring_p)
            two = (Direct if straight & 2 else Scatter)(remote, 6, halves, *coded("second"), 64 * p, 16, s, ring_s)
            back_two = gather(straight & 2, 14, pre, 64 * p, 16, s, ring_s)
            back_one = gather(straight & 1, 20, pre, 0, 64, p, ring_p)
            row = 64 * p + 16 * s
            swap = remote(12, b["sent_y"], b["got_y"], across)

            def begin():
                load(k)
                for i in range(2):
                    part[i] = dot(qs[k], fac[k, pl.ds(col + i * h, h), :])
                one.first()

            def third():
                two.last()
                for i in range(2):
                    put(b["sent_y"].at[i], halves[i], row, 16)
                swap.start()

            def fourth():
                swap.wait()
                rows = pl.ds(aligned(row), 16)
                for i in range(2):
                    pre[i, rows, :] = ((part[i, rows, :] + decode(b["got_y"][i])) * (1.0 / SCALE)).astype(BF16)
                back_two.first()

            return [
                [begin], [one.second], [one.last, two.first], [two.second], [third], [fourth],
                [back_two.second], [back_two.last, back_one.first], [back_one.second],
                [back_one.last, lambda: finish(u)],
            ]
        if kind == 1:
            one = Scatter(remote, 0, halves, *coded("second"), 0, 64, s, ring_s)
            two = Direct(remote, 6, halves, *coded("first"), 64 * s, 16, p, ring_p)
            back_two = DirectGather(remote, 9, pre.at[y], 64 * s, 16, p, ring_p)
            back_one = gather(straight & 1, 20, pre.at[y], 0, 64, s, ring_s)
            row = 64 * s + 16 * p
            swap = remote(13, pre.at[y], pre.at[y], across)

            def store():
                rows = pl.ds(aligned(row), 16)
                for i in range(2):
                    pre[y, i, rows, :] = (part[i, rows, :] * (1.0 / SCALE)).astype(BF16)

            return [
                [lambda: send_rows(u)], [lambda: sum_rows(u), one.first], [one.second],
                [one.last, two.first], [two.last, store, back_two.first], [back_two.last, back_one.first],
                [back_one.second], [back_one.last, swap.start], [swap.wait, lambda: finish(u)],
            ]
        one = Scatter(remote, 0, halves, *coded("first"), 0, 64, p, ring_p)
        two = (Direct if straight & 2 else Scatter)(remote, 6, halves, *coded("second"), 64 * p, 16, s, ring_s)
        back_two = gather(straight & 2, 14, pre, 64 * p, 16, s, ring_s)
        back_one = gather(straight & 1, 20, pre, 0, 64, p, ring_p)
        rows = pl.ds(aligned(64 * p + 16 * s), 16)
        swap = remote(13, pre.at[y, rows, :], pre.at[y, rows, :], across)

        def store():
            for i in range(2):
                pre[y, rows, pl.ds(i * q, q)] = (part[i, rows, :] * (1.0 / SCALE)).astype(BF16)

        return [
            [lambda: send_rows(u)], [lambda: sum_rows(u), one.first], [one.second], [one.last, two.first],
            [two.second], [two.last, store, swap.start], [swap.wait, back_two.first], [back_two.second],
            [back_two.last, back_one.first], [back_one.second], [back_one.last, lambda: finish(u)],
        ]

    steps = [[acts for acts in steps_of(u) if acts != [None]] for u in range(len(UNITS))]
    pl.semaphore_wait(barrier, len(everyone))
    for i, u in enumerate(ORDER):
        for act in steps[u].pop(0):
            act()
        if i in (LATE, LATE + 4):
            inp_copy((i - LATE) // 4).start()

    def fin_copy(d):
        who = (lay + d) % 4
        src = fin.at[pl.ds(pl.multiple_of(8 * who, 8), 8), :]
        return Remote(log, (fin_send, fin_recv), d - 1, src, rfin.at[d - 1], (who, tok))

    for d in (2, 3, 1):
        fin_copy(d).start()
    for c in log:
        c.wait_send()
    total = fin[pl.ds(pl.multiple_of(8 * lay, 8), 8), :]
    for d in (1, 2, 3):
        fin_copy(d).wait()
        total = total + rfin[d - 1]
    out_ref[...] = total


def local(inputs, out_grads, a_inverse, g_inverse, query_in, query_out):
    layers, tokens, width = inputs.shape
    depth = a_inverse.shape[2]
    rows = query_in.shape[1] * query_in.shape[2]
    dma = pltpu.SemaphoreType.DMA
    vmem = pltpu.VMEM
    scratch = [
        vmem((SLABS, rows, depth), BF16), vmem((SLABS, rows, depth), BF16),
        vmem((SLABS, width, depth), BF16), vmem((2, tokens, width), BF16),
        vmem((2, tokens, rows), F32), vmem((32, tokens), F32), vmem((3, 8, tokens), F32),
        dma((SLABS,)), dma((SLABS,)), dma((SLABS,)), dma((SLABS,)), dma((3,)), dma((3,)),
    ]
    for _, kind, _, w, straight in UNITS:
        for shape, dtype in unit_scratch(kind, w, straight).values():
            scratch.append(dma(shape) if dtype is None else vmem(shape, dtype))
    hbm = pl.BlockSpec(memory_space=pl.ANY)
    near = pl.BlockSpec(memory_space=pltpu.VMEM)
    scores = pl.pallas_call(
        kernel,
        out_shape=jax.ShapeDtypeStruct((8, tokens), F32),
        in_specs=[near, near, hbm, hbm, hbm, hbm],
        out_specs=near,
        scratch_shapes=scratch,
        compiler_params=pltpu.CompilerParams(
            collective_id=1, has_side_effects=True, vmem_limit_bytes=60 * 2**20
        ),
        cost_estimate=pl.CostEstimate(flops=6 * 10**9, bytes_accessed=26 * 10**6, transcendentals=0),
        name="influence",
    )(
        query_in.reshape(layers, rows, depth), query_out.reshape(layers, rows, depth),
        a_inverse, g_inverse, inputs, out_grads,
    )
    return scores.T


def solution(mesh):
    in_specs = (
        P("layer", "tok", None),
        P("layer", "tok", None),
        P("layer", None, "tok"),
        P("layer", None, "tok"),
        P("layer", None, None, "tok"),
        P("layer", None, None, "tok"),
    )
    return jax.shard_map(
        local, mesh=mesh, in_specs=in_specs, out_specs=P("tok", "layer"), check_vma=False
    )
```
